32 devices in a mesh: gx: 4 (over z), gy: 4 (over y, x), gz: 2 (over core).
Axes of the slice: x: 2, y: 2, z: 4, core: 2. Of those that a mesh axis runs over, the one named last changes fastest.
Arguments:
- fields: float32 [40, 32, 64, 256], P(None, 'gx', 'gy', 'gz'), may hold values from 0.1 to 1.5
- source: float32 [40, 32, 64, 256], P(None, 'gx', 'gy', 'gz'), may hold values from 0.005 to 0.2
- velocity: float32 [3, 32, 64, 256], P(None, 'gx', 'gy', 'gz'), may hold values from -1 to 1
- diffusivity: float32 [40], replicated, may hold values from 0.02 to 0.09
- reacting: int32 [32, 64, 2], P('gx', 'gy', 'gz'), may hold values from 0 to 1, as said below
- counts: int32 [32, 64, 2], P('gx', 'gy', 'gz'), may hold values from 1 to 4
- mechanism: int32 [4, 100], replicated, may hold values from 0 to 21
- prefactor: float32 [100], replicated, may hold values from 0.5 to 5
- activation: float32 [100], replicated, may hold values from 0.3 to 3
- heat_release: float32 [100], replicated, may hold values from 0.01 to 0.1
Outputs:
- evolved: float32 [40, 32, 64, 256], P(None, 'gx', 'gy', 'gz')
The draws below stay inside these ranges and needn't reach their ends.
Inputs may be any that keep to these rules, and one draw needn't show every extreme that they name: `reacting`: over all devices exactly 512 blocks react, and on one device all of its 128 blocks react.
All inputs are finite; a program needn't handle non-finite values.
Results may differ from the reference program's by a relative error of at most 0.0003.
Values sent between devices are 32-bit elements; how exact they have to be, the bound alone decides.
A program may use at most 128 MiB of HBM per device.

```python
import math
import jax
import jax.numpy as jnp
from jax import lax

FIELDS = 40
SPECIES = 22
REACTIONS = 100
CZ = 128
SUB = 4
CX = 8
CY = 16
NX = 32
NY = 64
NZ = 256
CAP = 16
N_GZ = 2


def draw_reacting(key, part):
    along_x = NX // CX
    along_y = NY // CY
    layers = NZ // CZ
    devices = along_x * along_y * layers
    all_blocks = NX * NY * layers
    key_level, key_top, key_jitter = jax.random.split(key, 3)
    x_index = lax.broadcasted_iota(jnp.int32, (NX, NY, layers), 0)
    y_index = lax.broadcasted_iota(jnp.int32, (NX, NY, layers), 1)
    z_index = lax.broadcasted_iota(jnp.int32, (NX, NY, layers), 2)
    owners = x_index // CX * (along_y * layers) + y_index // CY * layers + z_index
    levels = jax.random.randint(key_level, (devices,), 0, 4)
    busiest = jax.random.randint(key_top, (), 0, devices)
    levels = jnp.where(jnp.arange(devices, dtype=jnp.int32) == busiest, 16, levels)
    jitter = jax.random.randint(key_jitter, (NX, NY, layers), 0, 1024)
    scores = (jnp.take(levels, owners) * 256 + jitter).reshape(-1) * all_blocks + jnp.arange(all_blocks, dtype=jnp.int32)
    wanted = CAP * devices
    ranking = jnp.argsort(-scores)
    placed = jnp.zeros((all_blocks,), jnp.int32).at[ranking].set(jnp.arange(all_blocks, dtype=jnp.int32))
    return (placed < wanted).astype(jnp.int32).reshape(NX, NY, layers)


def plant(values, rng, low, high):
    dims = values.shape
    spot = [jax.random.randint(jax.random.fold_in(rng, axis), (), 0, dims[axis]) for axis in range(len(dims))]
    values = values.at[tuple(spot)].set(low)
    longest = dims.index(max(dims))
    spot[longest] = (spot[longest] + 1) % dims[longest]
    return values.at[tuple(spot)].set(high)


def level_of(rng, extent, shards, low, high):
    loudness = 1.0
    for position, shards_of in shards:
        steps = jax.random.uniform(jax.random.fold_in(jax.random.fold_in(rng, 6), position), (shards_of,), jnp.float32, low / len(shards), high / len(shards))
        loudness = loudness * jnp.repeat(jnp.exp(steps), extent[position] // shards_of).reshape((-1,) + (1,) * (len(extent) - 1 - position))
    return loudness


def setup_inputs(seed: int = 0) -> dict:
    key_of = jax.random.split(jax.random.key(seed), 11)
    return {
        "fields": jnp.clip(jnp.exp(math.log(1.5) - 2.7080502 * jax.random.uniform(key_of[0], (FIELDS, NX, NY, NZ), jnp.float32) ** level_of(key_of[0], (FIELDS, NX, NY, NZ), ((1, 4), (2, 4), (3, 2)), -0.2, 0.2)), 0.1, 1.5),
        "source": jnp.clip(jnp.exp(math.log(0.2) - 3.6888795 * jax.random.uniform(key_of[1], (FIELDS, NX, NY, NZ), jnp.float32) ** level_of(key_of[1], (FIELDS, NX, NY, NZ), ((1, 4), (2, 4), (3, 2)), -0.2, 0.2)), 0.005, 0.2),
        "velocity": jnp.clip(jax.random.uniform(key_of[2], (3, NX, NY, NZ), jnp.float32, -1.0, 1.0) * level_of(key_of[2], (3, NX, NY, NZ), ((1, 4), (2, 4), (3, 2)), -0.4, 0.0), -1.0, 1.0),
        "diffusivity": jnp.clip(jnp.exp(jax.random.uniform(key_of[3], (FIELDS,), jnp.float32, math.log(0.02), math.log(0.09))), 0.02, 0.09),
        "reacting": draw_reacting(jax.random.fold_in(key_of[10], 71), 0),
        "counts": plant(jax.random.randint(key_of[5], (NX, NY, N_GZ), 1, SUB + 1), jax.random.fold_in(key_of[5], 1), 1, SUB).astype(jnp.int32),
        "mechanism": plant(jax.random.randint(key_of[6], (4, REACTIONS), 0, SPECIES), jax.random.fold_in(key_of[6], 1), 0, SPECIES - 1).astype(jnp.int32),
        "prefactor": jnp.clip(jnp.exp(jax.random.uniform(key_of[7], (REACTIONS,), jnp.float32, math.log(0.5), math.log(5.0))), 0.5, 5.0),
        "activation": jnp.clip(jnp.exp(jax.random.uniform(key_of[8], (REACTIONS,), jnp.float32, math.log(0.3), math.log(3.0))), 0.3, 3.0),
        "heat_release": jnp.clip(jnp.exp(jax.random.uniform(key_of[9], (REACTIONS,), jnp.float32, math.log(0.01), math.log(0.1))), 0.01, 0.1),
    }


courant = 0.15
chem_step = 0.25


def advance(fields, velocity, diffusivity, source):
    padded = jnp.pad(fields, ((0, 0), (1, 1), (1, 1), (1, 1)))
    up_cells = (padded[:, 2:, 1:-1, 1:-1], padded[:, 1:-1, 2:, 1:-1], padded[:, 1:-1, 1:-1, 2:])
    down_cells = (padded[:, :-2, 1:-1, 1:-1], padded[:, 1:-1, :-2, 1:-1], padded[:, 1:-1, 1:-1, :-2])
    diffuse = diffusivity[:, None, None, None]
    result = fields + source
    for direction in range(3):
        flow_speed = velocity[direction][None]
        result = result - courant * (jnp.maximum(flow_speed, 0.0) * (fields - down_cells[direction]) + jnp.minimum(flow_speed, 0.0) * (up_cells[direction] - fields))
        result = result + diffuse * (up_cells[direction] + down_cells[direction] - 2.0 * fields)
    return result


def react(chem_state, sub_counts, mechanism, prefactor, activation, heat_release):
    species_row = lax.broadcasted_iota(jnp.int32, (1, SPECIES), 1)
    species_col = lax.broadcasted_iota(jnp.int32, (SPECIES, 1), 0)
    reactant_ids = mechanism[0:2].reshape(-1).astype(jnp.int32)
    takers = (reactant_ids[:, None] == species_row).astype(jnp.float32)
    losers = jnp.transpose(takers)
    makers = (mechanism[2][None, :] == species_col).astype(jnp.float32) + (mechanism[3][None, :] == species_col).astype(jnp.float32)
    makers = jnp.concatenate([makers, heat_release[None, :].astype(jnp.float32)], 0)
    interval = chem_step / sub_counts.astype(jnp.float32)
    for substep in range(SUB):
        fractions = chem_state[:SPECIES]
        temper = chem_state[SPECIES]
        rate_const = prefactor[:, None, None] * jnp.exp(-activation[:, None, None] / temper[None])
        paired = jnp.take(fractions, reactant_ids, axis=0)
        reactant_one = paired[:REACTIONS]
        reactant_two = paired[REACTIONS:]
        progress = rate_const * reactant_one * reactant_two
        loss_rate = jnp.einsum("kj,jnc->knc", losers, jnp.concatenate([rate_const * reactant_two, rate_const * reactant_one], 0), precision=lax.Precision.HIGHEST)
        gain_rate = jnp.einsum("kj,jnc->knc", makers, progress, precision=lax.Precision.HIGHEST)
        widths = interval[None, :, None]
        renewed_fractions = (fractions + widths * gain_rate[:SPECIES]) / (1.0 + widths * loss_rate)
        renewed_temper = temper + interval[:, None] * gain_rate[SPECIES]
        renewed = jnp.concatenate([renewed_fractions, renewed_temper[None]], 0)
        chem_state = jnp.where((substep < sub_counts)[None, :, None], renewed, chem_state)
    return chem_state


def reference(fields, source, velocity, diffusivity, reacting, counts, mechanism, prefactor, activation, heat_release):
    current = fields
    for substep in range(2):
        current = advance(current, velocity, diffusivity, source)
    blocks = current.reshape(FIELDS, NX, NY * N_GZ, CZ)
    chemistry = jnp.moveaxis(blocks[:SPECIES + 1], 1, 0)
    marked_rows = reacting.reshape(NX, NY * N_GZ)
    count_rows = counts.reshape(NX, NY * N_GZ)

    def one_row(items):
        chem_state, marked, sub_counts = items
        reacted_row = react(chem_state, sub_counts, mechanism, prefactor, activation, heat_release)
        return jnp.where((marked == 1)[None, :, None], reacted_row, chem_state)

    reacted = lax.map(one_row, (chemistry, marked_rows, count_rows))
    merged = jnp.concatenate([jnp.moveaxis(reacted, 0, 1), blocks[SPECIES + 1:]], 0)
    return merged.reshape(FIELDS, NX, NY, NZ)
```

```python
import functools
import math

import jax
import jax.numpy as jnp
from jax import lax
from jax.experimental import pallas as pl
from jax.experimental.pallas import tpu as pltpu
from jax.sharding import PartitionSpec as P

COURANT = 0.15
CHEM_STEP = 0.25
CHUNK = 8
GROUP = 8
MESH = pl.DeviceIdType.MESH


def transport_kernel(
    sizes,
    diff_ref,
    fields_ref,
    source_ref,
    vel_ref,
    out_ref,
    mid_ref,
    coef,
    xlo,
    xhi,
    ylo,
    yhi,
    zlo,
    zhi,
    zsend,
    send_sem,
    recv_sem,
):
    nf, cx, cy, cz = fields_ref.shape
    chunks = nf // CHUNK
    axes = ("gx", "gy", "gz")
    where = [lax.axis_index(a) for a in axes]
    has_prev = [w > 0 for w in where]
    has_next = [w < n - 1 for w, n in zip(where, sizes)]

    def target(d):
        a = d // 2
        return {axes[a]: where[a] + (1 if d % 2 == 0 else -1)}

    def sends(d):
        return has_next[d // 2] if d % 2 == 0 else has_prev[d // 2]

    def receives(d):
        return has_prev[d // 2] if d % 2 == 0 else has_next[d // 2]

    def copy(step, c, d):
        src = fields_ref if step == 0 else mid_ref
        fs = pl.ds(c * CHUNK, CHUNK)
        if d == 0:
            pair = (src.at[fs, cx - 1], xlo.at[step, fs])
        elif d == 1:
            pair = (src.at[fs, 0], xhi.at[step, fs])
        elif d == 2:
            pair = (src.at[fs, :, cy - 1], ylo.at[step, fs])
        elif d == 3:
            pair = (src.at[fs, :, 0], yhi.at[step, fs])
        elif d == 4:
            pair = (zsend.at[step, c], zlo.at[step, c])
        else:
            pair = (zsend.at[step, c], zhi.at[step, c])
        return pltpu.make_async_remote_copy(
            src_ref=pair[0],
            dst_ref=pair[1],
            send_sem=send_sem.at[step, c, d],
            recv_sem=recv_sem.at[step, c, d],
            device_id=target(d),
            device_id_type=MESH,
        )

    def start(step, c, d):
        @pl.when(sends(d))
        def _():
            copy(step, c, d).start()

    lane = lax.broadcasted_iota(jnp.int32, (cx, cy, cz), 2)

    def pack_z(value, i, packed):
        packed = jnp.where(lane == i, pltpu.roll(value, i + 1, 2), packed)
        return jnp.where(
            lane == cz // 2 + i, pltpu.roll(value, cz // 2 + i, 2), packed
        )

    for d, ref in enumerate((xlo, xhi, ylo, yhi, zlo, zhi)):

        @pl.when(jnp.logical_not(receives(d)))
        def _(ref=ref):
            ref[...] = jnp.zeros_like(ref)

    barrier = pltpu.get_barrier_semaphore()
    for d in range(6):

        @pl.when(sends(d))
        def _(d=d):
            pl.semaphore_signal(
                barrier, inc=1, device_id=target(d), device_id_type=MESH
            )

    arriving = sum(receives(d).astype(jnp.int32) for d in range(6))
    pl.semaphore_wait(barrier, arriving)

    def first(c, _):
        for d in range(4):
            start(0, c, d)
        return 0

    lax.fori_loop(0, chunks, first, 0)

    def first_z(c, _):
        packed = jnp.zeros((cx, cy, cz), jnp.float32)
        for i in range(CHUNK):
            packed = pack_z(fields_ref[c * CHUNK + i], i, packed)
        zsend[0, c] = packed
        for d in (4, 5):
            start(0, c, d)
        return 0

    lax.fori_loop(0, chunks, first_z, 0)

    total = jnp.ones((cx, cy, cz), jnp.float32)
    for a in range(3):
        up = COURANT * jnp.maximum(vel_ref[a], 0.0)
        down = -COURANT * jnp.minimum(vel_ref[a], 0.0)
        coef[2 * a] = up
        coef[2 * a + 1] = down
        total = total - up - down
    coef[6] = total

    row = lax.broadcasted_iota(jnp.int32, (cy, cz), 0)
    col = lax.broadcasted_iota(jnp.int32, (cy, cz), 1)

    def substep(step):
        src = fields_ref if step == 0 else mid_ref
        dst = mid_ref if step == 0 else out_ref

        def chunk(c, _):
            for d in range(6):

                @pl.when(receives(d))
                def _(d=d):
                    copy(step, c, d).wait_recv()

            def one(i, _):
                f = c * CHUNK + i
                diffuse = diff_ref[f]
                for x in range(cx):
                    here = src[f, x]
                    x_dn = src[f, x - 1] if x > 0 else xlo[step, f]
                    x_up = src[f, x + 1] if x < cx - 1 else xhi[step, f]
                    y_dn = jnp.where(
                        row == 0, ylo[step, f, pl.ds(x, 1)], pltpu.roll(here, 1, 0)
                    )
                    y_up = jnp.where(
                        row == cy - 1,
                        yhi[step, f, pl.ds(x, 1)],
                        pltpu.roll(here, cy - 1, 0),
                    )
                    z_dn = jnp.where(
                        col == 0,
                        pltpu.roll(zlo[step, c, x], lax.rem(cz - i, cz), 1),
                        pltpu.roll(here, 1, 1),
                    )
                    z_up = jnp.where(
                        col == cz - 1,
                        pltpu.roll(zhi[step, c, x], cz // 2 - 1 - i, 1),
                        pltpu.roll(here, cz - 1, 1),
                    )
                    flow = here * coef[6, x]
                    around = here * -6.0
                    for a, (dn, up) in enumerate(
                        ((x_dn, x_up), (y_dn, y_up), (z_dn, z_up))
                    ):
                        flow = flow + (dn * coef[2 * a, x] + up * coef[2 * a + 1, x])
                        around = around + (dn + up)
                    dst[f, x] = source_ref[f, x] + flow + diffuse * around
                return 0

            lax.fori_loop(0, CHUNK, one, 0)
            if step == 0:
                packed = jnp.zeros((cx, cy, cz), jnp.float32)
                for i in range(CHUNK):
                    packed = pack_z(mid_ref[c * CHUNK + i], i, packed)
                zsend[1, c] = packed
                for d in range(6):
                    start(1, c, d)
            return 0

        lax.fori_loop(0, chunks, chunk, 0)

    substep(0)
    substep(1)

    def finish(c, _):
        for step in range(2):
            for d in range(6):

                @pl.when(sends(d))
                def _(d=d, step=step):
                    copy(step, c, d).wait_send()

        return 0

    lax.fori_loop(0, chunks, finish, 0)


def transport(fields, source, velocity, diffusivity):
    nf, cx, cy, cz = fields.shape
    chunks = nf // CHUNK
    sizes = tuple(lax.axis_size(a) for a in ("gx", "gy", "gz"))
    f32 = jnp.float32
    vmem = pl.BlockSpec(memory_space=pltpu.VMEM)
    return pl.pallas_call(
        functools.partial(transport_kernel, sizes),
        out_shape=jax.ShapeDtypeStruct(fields.shape, f32),
        in_specs=[pl.BlockSpec(memory_space=pltpu.SMEM), vmem, vmem, vmem],
        out_specs=vmem,
        scratch_shapes=[
            pltpu.VMEM((nf, cx, cy, cz), f32),
            pltpu.VMEM((7, cx, cy, cz), f32),
            pltpu.VMEM((2, nf, cy, cz), f32),
            pltpu.VMEM((2, nf, cy, cz), f32),
            pltpu.VMEM((2, nf, cx, cz), f32),
            pltpu.VMEM((2, nf, cx, cz), f32),
            pltpu.VMEM((2, chunks, cx, cy, cz), f32),
            pltpu.VMEM((2, chunks, cx, cy, cz), f32),
            pltpu.VMEM((2, chunks, cx, cy, cz), f32),
            pltpu.SemaphoreType.DMA((2, chunks, 6)),
            pltpu.SemaphoreType.DMA((2, chunks, 6)),
        ],
        compiler_params=pltpu.CompilerParams(
            collective_id=0, has_side_effects=True, vmem_limit_bytes=48 * 2**20
        ),
    )(diffusivity, fields, source, velocity)


def chemistry_kernel(
    order_ref,
    count_ref,
    mech_ref,
    rates_ref,
    state_ref,
    out_ref,
    gather_ref,
    scatter_ref,
    act_ref,
    pre_ref,
):
    blocks = order_ref.shape[0]
    lanes = mech_ref.shape[1]
    reac = gather_ref.shape[0] // 2
    rows = scatter_ref.shape[0] // 2
    species = rows - 2
    out_ref[...] = state_ref[...]

    sub = lax.broadcasted_iota(jnp.int32, (rows, lanes), 0)
    hot = [(mech_ref[pl.ds(i, 1), :] == sub).astype(jnp.float32) for i in range(4)]
    heat = rates_ref[pl.ds(2, 1), :]
    heat_hi = heat.astype(jnp.bfloat16).astype(jnp.float32)
    made = hot[2] + hot[3]
    made = jnp.where(sub == species, heat_hi, made)
    made = jnp.where(sub == species + 1, heat - heat_hi, made)
    none = jnp.zeros((rows, reac), jnp.float32)
    lost = jnp.concatenate([hot[0][:, :reac], hot[1][:, :reac], none], 1)
    gain = jnp.concatenate([none, none, made[:, :reac]], 1)
    scatter_ref[...] = jnp.concatenate([lost, gain], 0).astype(jnp.bfloat16)
    spare = jnp.zeros((lanes - rows, lanes), jnp.float32)
    for i in range(2):
        turned = jnp.concatenate([hot[i], spare], 0).T[:reac, :rows]
        gather_ref[pl.ds(i * reac, reac), :] = jnp.concatenate(
            [turned, turned, turned], 1
        ).astype(jnp.bfloat16)
    cols = jnp.concatenate(
        [rates_ref[...], jnp.zeros((lanes - rates_ref.shape[0], lanes), jnp.float32)], 0
    ).T
    act_ref[...] = jnp.broadcast_to(cols[:reac, 0:1], act_ref.shape)
    pre_ref[...] = jnp.broadcast_to(cols[:reac, 1:2], pre_ref.shape)

    width = state_ref.shape[1]

    def group(g, _):
        ids = [order_ref[g * GROUP + i] for i in range(GROUP)]
        ns = [count_ref[g * GROUP + i] for i in range(GROUP)]
        states = tuple(out_ref[pl.ds(b, rows, stride=blocks), :] for b in ids)

        def step(s, states):
            new = []
            for i in range(GROUP):
                y = states[i]
                n = ns[i]
                wide = CHEM_STEP / jnp.full((rows, width), n, jnp.int32).astype(
                    jnp.float32
                )
                hi = y.astype(jnp.bfloat16)
                rest = y - hi.astype(jnp.float32)
                mid = rest.astype(jnp.bfloat16)
                low = (rest - mid.astype(jnp.float32)).astype(jnp.bfloat16)
                pair = jnp.dot(
                    gather_ref[...],
                    jnp.concatenate([hi, mid, low], 0),
                    preferred_element_type=jnp.float32,
                )
                inverse = 1.0 / y[species : species + 1]
                k = pre_ref[...] * jnp.exp2(act_ref[...] * inverse)
                one = k * pair[:reac]
                two = k * pair[reac:]
                q = one * pair[reac:]
                terms = jnp.concatenate([two, one, q], 0).astype(jnp.bfloat16)
                sums = jnp.dot(
                    scatter_ref[...], terms, preferred_element_type=jnp.float32
                )
                loss = sums[:rows]
                gain = sums[rows:]
                fresh = (y + wide * gain) / (1.0 + wide * loss)
                warm = y[species : species + 1] + wide[:1] * (
                    gain[species : species + 1] + gain[species + 1 : species + 2]
                )
                rid = lax.broadcasted_iota(jnp.int32, (rows, width), 0)
                fresh = jnp.where(rid == species, warm, fresh)
                keep = jnp.logical_or(rid == species + 1, s >= n)
                new.append(jnp.where(keep, y, fresh))
            return tuple(new)

        most = ns[0]
        for n in ns[1:]:
            most = jnp.maximum(most, n)
        states = lax.fori_loop(0, most, step, states)
        for b, y in zip(ids, states):
            out_ref[pl.ds(b, rows, stride=blocks), :] = y
        return 0

    def busy(g):
        return jnp.logical_and(
            g < blocks // GROUP,
            count_ref[jnp.minimum(g * GROUP, blocks - 1)] > 0,
        )

    lax.while_loop(busy, lambda g: (group(g, 0), g + 1)[1], 0)


def chemistry(state, reacting, counts, mechanism, prefactor, activation, heat_release):
    nf, cx, cy, cz = state.shape
    blocks = cx * cy
    reactions = prefactor.shape[0]
    lanes = 128
    reac = -(-reactions // 8) * 8
    rows = 24
    todo = (reacting * counts).reshape(blocks)
    index = jnp.arange(blocks, dtype=jnp.int32)
    ahead = (todo[None, :] > todo[:, None]) | (
        (todo[None, :] == todo[:, None]) & (index[None, :] < index[:, None])
    )
    rank = jnp.sum(ahead.astype(jnp.int32), 1)
    placed = rank[None, :] == index[:, None]
    order = jnp.sum(jnp.where(placed, index[None, :], 0), 1)
    sorted_counts = jnp.sum(jnp.where(placed, todo[None, :], 0), 1)
    pad = ((0, 0), (0, lanes - reactions))
    mech = jnp.pad(mechanism, ((0, 4), (0, lanes - reactions)))
    rates = jnp.stack([activation * -math.log2(math.e), prefactor, heat_release])
    rates = jnp.pad(rates, ((0, 5), pad[1]))
    vmem = pl.BlockSpec(memory_space=pltpu.VMEM)
    smem = pl.BlockSpec(memory_space=pltpu.SMEM)
    flat = state.reshape(nf * blocks, cz)
    out = pl.pallas_call(
        chemistry_kernel,
        out_shape=jax.ShapeDtypeStruct(flat.shape, jnp.float32),
        in_specs=[smem, smem, vmem, vmem, vmem],
        out_specs=vmem,
        scratch_shapes=[
            pltpu.VMEM((2 * reac, 3 * rows), jnp.bfloat16),
            pltpu.VMEM((2 * rows, 3 * reac), jnp.bfloat16),
            pltpu.VMEM((reac, cz), jnp.float32),
            pltpu.VMEM((reac, cz), jnp.float32),
        ],
        compiler_params=pltpu.CompilerParams(vmem_limit_bytes=48 * 2**20),
    )(order, sorted_counts, mech, rates, flat)
    return out.reshape(state.shape)


def body(
    fields,
    source,
    velocity,
    diffusivity,
    reacting,
    counts,
    mechanism,
    prefactor,
    activation,
    heat_release,
):
    moved = transport(fields, source, velocity, diffusivity)
    return chemistry(
        moved, reacting, counts, mechanism, prefactor, activation, heat_release
    )


def solution(mesh):
    grid = P(None, "gx", "gy", "gz")
    placed = (grid, grid, grid, P(), P("gx", "gy", "gz"), P("gx", "gy", "gz"))
    return jax.shard_map(
        body,
        mesh=mesh,
        in_specs=placed + (P(),) * 4,
        out_specs=grid,
        check_vma=False,
    )
```

```python
import functools
import math

import jax
import jax.numpy as jnp
from jax import lax
from jax.experimental import pallas as pl
from jax.experimental.pallas import tpu as pltpu
from jax.sharding import PartitionSpec as P

COURANT = 0.15
CHEM_STEP = 0.25
CHUNK = 8
GROUP = 32
MESH = pl.DeviceIdType.MESH


def transport_kernel(
    sizes,
    diff_ref,
    fields_ref,
    source_ref,
    vel_ref,
    out_ref,
    mid_ref,
    coef,
    xlo,
    xhi,
    ylo,
    yhi,
    zlo,
    zhi,
    zsend,
    send_sem,
    recv_sem,
):
    nf, cx, cy, cz = fields_ref.shape
    chunks = nf // CHUNK
    axes = ("gx", "gy", "gz")
    where = [lax.axis_index(a) for a in axes]
    has_prev = [w > 0 for w in where]
    has_next = [w < n - 1 for w, n in zip(where, sizes)]

    def target(d):
        a = d // 2
        return {axes[a]: where[a] + (1 if d % 2 == 0 else -1)}

    def sends(d):
        return has_next[d // 2] if d % 2 == 0 else has_prev[d // 2]

    def receives(d):
        return has_prev[d // 2] if d % 2 == 0 else has_next[d // 2]

    def copy(step, c, d):
        src = fields_ref if step == 0 else mid_ref
        fs = pl.ds(c * CHUNK, CHUNK)
        if d == 0:
            pair = (src.at[fs, cx - 1], xlo.at[step, fs])
        elif d == 1:
            pair = (src.at[fs, 0], xhi.at[step, fs])
        elif d == 2:
            pair = (src.at[fs, :, cy - 1], ylo.at[step, fs])
        elif d == 3:
            pair = (src.at[fs, :, 0], yhi.at[step, fs])
        elif d == 4:
            pair = (zsend.at[step, c], zlo.at[step, c])
        else:
            pair = (zsend.at[step, c], zhi.at[step, c])
        return pltpu.make_async_remote_copy(
            src_ref=pair[0],
            dst_ref=pair[1],
            send_sem=send_sem.at[step, c, d],
            recv_sem=recv_sem.at[step, c, d],
            device_id=target(d),
            device_id_type=MESH,
        )

    def start(step, c, d):
        @pl.when(sends(d))
        def _():
            copy(step, c, d).start()

    lane = lax.broadcasted_iota(jnp.int32, (cx, cy, cz), 2)

    def pack_z(value, i, packed):
        packed = jnp.where(lane == i, pltpu.roll(value, i + 1, 2), packed)
        return jnp.where(
            lane == cz // 2 + i, pltpu.roll(value, cz // 2 + i, 2), packed
        )

    for d, ref in enumerate((xlo, xhi, ylo, yhi, zlo, zhi)):

        @pl.when(jnp.logical_not(receives(d)))
        def _(ref=ref):
            ref[...] = jnp.zeros_like(ref)

    barrier = pltpu.get_barrier_semaphore()
    for d in range(6):

        @pl.when(sends(d))
        def _(d=d):
            pl.semaphore_signal(
                barrier, inc=1, device_id=target(d), device_id_type=MESH
            )

    arriving = sum(receives(d).astype(jnp.int32) for d in range(6))
    pl.semaphore_wait(barrier, arriving)

    def first(c, _):
        for d in range(4):
            start(0, c, d)
        return 0

    lax.fori_loop(0, chunks, first, 0)

    def first_z(c, _):
        packed = jnp.zeros((cx, cy, cz), jnp.float32)
        for i in range(CHUNK):
            packed = pack_z(fields_ref[c * CHUNK + i], i, packed)
        zsend[0, c] = packed
        for d in (4, 5):
            start(0, c, d)
        return 0

    lax.fori_loop(0, chunks, first_z, 0)

    total = jnp.ones((cx, cy, cz), jnp.float32)
    for a in range(3):
        up = COURANT * jnp.maximum(vel_ref[a], 0.0)
        down = -COURANT * jnp.minimum(vel_ref[a], 0.0)
        coef[2 * a] = up
        coef[2 * a + 1] = down
        total = total - up - down
    coef[6] = total

    row = lax.broadcasted_iota(jnp.int32, (cy, cz), 0)
    col = lax.broadcasted_iota(jnp.int32, (cy, cz), 1)

    def substep(step):
        src = fields_ref if step == 0 else mid_ref
        dst = mid_ref if step == 0 else out_ref

        def chunk(c, _):
            for d in range(6):

                @pl.when(receives(d))
                def _(d=d):
                    copy(step, c, d).wait_recv()

            def one(i, _):
                f = c * CHUNK + i
                diffuse = diff_ref[f]
                for x in range(cx):
                    here = src[f, x]
                    x_dn = src[f, x - 1] if x > 0 else xlo[step, f]
                    x_up = src[f, x + 1] if x < cx - 1 else xhi[step, f]
                    y_dn = jnp.where(
                        row == 0, ylo[step, f, pl.ds(x, 1)], pltpu.roll(here, 1, 0)
                    )
                    y_up = jnp.where(
                        row == cy - 1,
                        yhi[step, f, pl.ds(x, 1)],
                        pltpu.roll(here, cy - 1, 0),
                    )
                    z_dn = jnp.where(
                        col == 0,
                        pltpu.roll(zlo[step, c, x], lax.rem(cz - i, cz), 1),
                        pltpu.roll(here, 1, 1),
                    )
                    z_up = jnp.where(
                        col == cz - 1,
                        pltpu.roll(zhi[step, c, x], cz // 2 - 1 - i, 1),
                        pltpu.roll(here, cz - 1, 1),
                    )
                    flow = here * coef[6, x]
                    around = here * -6.0
                    for a, (dn, up) in enumerate(
                        ((x_dn, x_up), (y_dn, y_up), (z_dn, z_up))
                    ):
                        flow = flow + (dn * coef[2 * a, x] + up * coef[2 * a + 1, x])
                        around = around + (dn + up)
                    dst[f, x] = source_ref[f, x] + flow + diffuse * around
                return 0

            lax.fori_loop(0, CHUNK, one, 0)
            if step == 0:
                packed = jnp.zeros((cx, cy, cz), jnp.float32)
                for i in range(CHUNK):
                    packed = pack_z(mid_ref[c * CHUNK + i], i, packed)
                zsend[1, c] = packed
                for d in range(6):
                    start(1, c, d)
            return 0

        lax.fori_loop(0, chunks, chunk, 0)

    substep(0)
    substep(1)

    def finish(c, _):
        for step in range(2):
            for d in range(6):

                @pl.when(sends(d))
                def _(d=d, step=step):
                    copy(step, c, d).wait_send()

        return 0

    lax.fori_loop(0, chunks, finish, 0)


def transport(fields, source, velocity, diffusivity):
    nf, cx, cy, cz = fields.shape
    chunks = nf // CHUNK
    sizes = tuple(lax.axis_size(a) for a in ("gx", "gy", "gz"))
    f32 = jnp.float32
    vmem = pl.BlockSpec(memory_space=pltpu.VMEM)
    return pl.pallas_call(
        functools.partial(transport_kernel, sizes),
        out_shape=jax.ShapeDtypeStruct(fields.shape, f32),
        in_specs=[pl.BlockSpec(memory_space=pltpu.SMEM), vmem, vmem, vmem],
        out_specs=vmem,
        scratch_shapes=[
            pltpu.VMEM((nf, cx, cy, cz), f32),
            pltpu.VMEM((7, cx, cy, cz), f32),
            pltpu.VMEM((2, nf, cy, cz), f32),
            pltpu.VMEM((2, nf, cy, cz), f32),
            pltpu.VMEM((2, nf, cx, cz), f32),
            pltpu.VMEM((2, nf, cx, cz), f32),
            pltpu.VMEM((2, chunks, cx, cy, cz), f32),
            pltpu.VMEM((2, chunks, cx, cy, cz), f32),
            pltpu.VMEM((2, chunks, cx, cy, cz), f32),
            pltpu.SemaphoreType.DMA((2, chunks, 6)),
            pltpu.SemaphoreType.DMA((2, chunks, 6)),
        ],
        compiler_params=pltpu.CompilerParams(
            collective_id=0, has_side_effects=True, vmem_limit_bytes=48 * 2**20
        ),
    )(diffusivity, fields, source, velocity)


def halves(value):
    hi = value.astype(jnp.bfloat16).astype(jnp.float32)
    return hi, value - hi


def chemistry_kernel(
    reactions,
    order_ref,
    count_ref,
    mech_ref,
    rates_ref,
    state_ref,
    out_ref,
    gather_ref,
    scatter_ref,
):
    blocks = order_ref.shape[0]
    lanes = mech_ref.shape[1]
    reac = gather_ref.shape[0]
    rows = scatter_ref.shape[0] // 2
    species = rows - 2
    out_ref[...] = state_ref[...]

    sub = lax.broadcasted_iota(jnp.int32, (rows, lanes), 0)
    hot = [(mech_ref[pl.ds(i, 1), :] == sub).astype(jnp.float32) for i in range(4)]
    act_hi, act_lo = halves(rates_ref[pl.ds(0, 1), :])
    real = lax.broadcasted_iota(jnp.int32, (1, lanes), 1) < reactions
    pre = jnp.where(real, jnp.log2(rates_ref[pl.ds(1, 1), :]), -3e4)
    pre_hi, pre_lo = halves(pre)
    heat_hi, heat_lo = halves(rates_ref[pl.ds(2, 1), :])

    def with_rows(base, one, two):
        base = jnp.where(sub == species, one, base)
        return jnp.where(sub == species + 1, two, base)

    used = hot[0] + hot[1]
    none = jnp.zeros((rows, lanes), jnp.float32)
    turned = jnp.concatenate(
        [
            with_rows(used, act_hi, pre_hi),
            with_rows(used, act_hi, 0.0),
            with_rows(none, act_lo, pre_lo),
            jnp.zeros((lanes - 3 * rows, lanes), jnp.float32),
        ],
        0,
    ).T
    gather_ref[...] = turned[:reac, : 3 * rows].astype(jnp.bfloat16)
    made = with_rows(hot[2] + hot[3], heat_hi, heat_lo)
    table = jnp.concatenate([used, made], 0)[:, :reac]
    scatter_ref[...] = jnp.concatenate([table, table], 1).astype(jnp.bfloat16)

    width = state_ref.shape[1]

    def group(g, _):
        ids = [order_ref[g * GROUP + i] for i in range(GROUP)]
        ns = [count_ref[g * GROUP + i] for i in range(GROUP)]
        state = jnp.concatenate(
            [out_ref[pl.ds(b, rows, stride=blocks), :] for b in ids], 1
        )
        count = jnp.concatenate([jnp.full((rows, width), n, jnp.int32) for n in ns], 1)
        wide = CHEM_STEP / jnp.maximum(count, 1).astype(jnp.float32)
        rid = lax.broadcasted_iota(jnp.int32, (rows, GROUP * width), 0)

        def step(s, y):
            logs = jnp.where(rid == species, 1.0 / y, jnp.log2(y))
            hi, lo = halves(jnp.where(rid == species + 1, 1.0, logs))
            q = jnp.exp2(
                jnp.dot(
                    gather_ref[...],
                    jnp.concatenate([hi, lo, hi], 0).astype(jnp.bfloat16),
                    preferred_element_type=jnp.float32,
                )
            )
            q_hi = q.astype(jnp.bfloat16)
            q_lo = (q - q_hi.astype(jnp.float32)).astype(jnp.bfloat16)
            sums = jnp.dot(
                scatter_ref[...],
                jnp.concatenate([q_hi, q_lo], 0),
                preferred_element_type=jnp.float32,
            )
            loss = sums[:rows]
            gain = sums[rows:]
            fresh = (y + wide * gain) * (y / (y + wide * loss))
            warm = y[species : species + 1] + wide[:1] * (
                gain[species : species + 1] + gain[species + 1 : species + 2]
            )
            fresh = jnp.where(rid == species, warm, fresh)
            keep = jnp.logical_or(rid == species + 1, s >= count)
            return jnp.where(keep, y, fresh)

        most = ns[0]
        for n in ns[1:]:
            most = jnp.maximum(most, n)
        state = lax.fori_loop(0, most, step, state)
        for i, b in enumerate(ids):
            out_ref[pl.ds(b, rows, stride=blocks), :] = state[
                :, i * width : (i + 1) * width
            ]
        return 0

    def busy(g):
        return jnp.logical_and(
            g < blocks // GROUP,
            count_ref[jnp.minimum(g * GROUP, blocks - 1)] > 0,
        )

    lax.while_loop(busy, lambda g: (group(g, 0), g + 1)[1], 0)


def chemistry(state, reacting, counts, mechanism, prefactor, activation, heat_release):
    nf, cx, cy, cz = state.shape
    blocks = cx * cy
    reactions = prefactor.shape[0]
    lanes = 128
    reac = -(-reactions // 16) * 16
    rows = 24
    todo = (reacting * counts).reshape(blocks)
    index = jnp.arange(blocks, dtype=jnp.int32)
    ahead = (todo[None, :] > todo[:, None]) | (
        (todo[None, :] == todo[:, None]) & (index[None, :] < index[:, None])
    )
    rank = jnp.sum(ahead.astype(jnp.int32), 1)
    placed = rank[None, :] == index[:, None]
    order = jnp.sum(jnp.where(placed, index[None, :], 0), 1)
    sorted_counts = jnp.sum(jnp.where(placed, todo[None, :], 0), 1)
    pad = ((0, 0), (0, lanes - reactions))
    mech = jnp.pad(mechanism, ((0, 4), (0, lanes - reactions)))
    rates = jnp.stack([activation * -math.log2(math.e), prefactor, heat_release])
    rates = jnp.pad(rates, ((0, 5), pad[1]))
    vmem = pl.BlockSpec(memory_space=pltpu.VMEM)
    smem = pl.BlockSpec(memory_space=pltpu.SMEM)
    flat = state.reshape(nf * blocks, cz)
    out = pl.pallas_call(
        functools.partial(chemistry_kernel, reactions),
        out_shape=jax.ShapeDtypeStruct(flat.shape, jnp.float32),
        in_specs=[smem, smem, vmem, vmem, vmem],
        out_specs=vmem,
        scratch_shapes=[
            pltpu.VMEM((reac, 3 * rows), jnp.bfloat16),
            pltpu.VMEM((2 * rows, 2 * reac), jnp.bfloat16),
        ],
        compiler_params=pltpu.CompilerParams(vmem_limit_bytes=48 * 2**20),
    )(order, sorted_counts, mech, rates, flat)
    return out.reshape(state.shape)


def body(
    fields,
    source,
    velocity,
    diffusivity,
    reacting,
    counts,
    mechanism,
    prefactor,
    activation,
    heat_release,
):
    moved = transport(fields, source, velocity, diffusivity)
    return chemistry(
        moved, reacting, counts, mechanism, prefactor, activation, heat_release
    )


def solution(mesh):
    grid = P(None, "gx", "gy", "gz")
    placed = (grid, grid, grid, P(), P("gx", "gy", "gz"), P("gx", "gy", "gz"))
    return jax.shard_map(
        body,
        mesh=mesh,
        in_specs=placed + (P(),) * 4,
        out_specs=grid,
        check_vma=False,
    )
```

```python
import functools
import math

import jax
import jax.numpy as jnp
from jax import lax
from jax.experimental import pallas as pl
from jax.experimental.pallas import tpu as pltpu
from jax.sharding import PartitionSpec as P

COURANT = 0.15
CHEM_STEP = 0.25
CHUNK = 8
GROUP = 32
MESH = pl.DeviceIdType.MESH


def ordered(todo):
    cx, cy = todo.shape
    blocks = cx * cy
    f32 = jnp.float32
    wide = jnp.concatenate([todo.astype(f32)] * cx, 1)
    shape = (cx, blocks)
    mine = lax.broadcasted_iota(jnp.int32, shape, 1) // cy == lax.broadcasted_iota(
        jnp.int32, shape, 0
    )
    row = jnp.sum(jnp.where(mine, wide, 0.0), 0, keepdims=True)
    down = lax.broadcasted_iota(jnp.int32, (blocks, blocks), 0)
    along = lax.broadcasted_iota(jnp.int32, (blocks, blocks), 1)
    col = jnp.sum(jnp.where(down == along, row, 0.0), 1, keepdims=True)
    ahead = (row > col) | ((row == col) & (along < down))
    rank = jnp.sum(jnp.where(ahead, 1.0, 0.0), 1, keepdims=True)
    value = down.astype(f32) + blocks * col
    placed = rank == along.astype(f32)
    return jnp.sum(jnp.where(placed, value, 0.0), 0, keepdims=True).astype(jnp.int32)


def transport_kernel(
    sizes,
    diff_hbm,
    fields_hbm,
    source_hbm,
    vel_hbm,
    reacting_ref,
    counts_ref,
    out_ref,
    plan_ref,
    diff_ref,
    fields_ref,
    source_ref,
    vel_ref,
    mid_ref,
    coef,
    xlo,
    xhi,
    ylo,
    yhi,
    zlo,
    zhi,
    zsend,
    send_sem,
    recv_sem,
    load_sem,
    once_sem,
):
    nf, cx, cy, cz = fields_hbm.shape
    chunks = nf // CHUNK
    axes = ("gx", "gy", "gz")
    where = [lax.axis_index(a) for a in axes]
    has_prev = [w > 0 for w in where]
    has_next = [w < n - 1 for w, n in zip(where, sizes)]

    def target(d):
        a = d // 2
        return {axes[a]: where[a] + (1 if d % 2 == 0 else -1)}

    def sends(d):
        return has_next[d // 2] if d % 2 == 0 else has_prev[d // 2]

    def receives(d):
        return has_prev[d // 2] if d % 2 == 0 else has_next[d // 2]

    def copy(step, c, d):
        src = fields_ref if step == 0 else mid_ref
        if step == 0 and d < 2:
            src = fields_hbm
        fs = pl.ds(c * CHUNK, CHUNK)
        if d == 0:
            pair = (src.at[fs, cx - 1], xlo.at[step, fs])
        elif d == 1:
            pair = (src.at[fs, 0], xhi.at[step, fs])
        elif d == 2:
            pair = (src.at[fs, :, cy - 1], ylo.at[step, fs])
        elif d == 3:
            pair = (src.at[fs, :, 0], yhi.at[step, fs])
        elif d == 4:
            pair = (zsend.at[step, c], zlo.at[step, c])
        else:
            pair = (zsend.at[step, c], zhi.at[step, c])
        return pltpu.make_async_remote_copy(
            src_ref=pair[0],
            dst_ref=pair[1],
            send_sem=send_sem.at[step, c, d],
            recv_sem=recv_sem.at[step, c, d],
            device_id=target(d),
            device_id_type=MESH,
        )

    def start(step, c, d):
        @pl.when(sends(d))
        def _():
            copy(step, c, d).start()

    lane = lax.broadcasted_iota(jnp.int32, (cx, cy, cz), 2)

    def pack_z(value, i, packed):
        packed = jnp.where(lane == i, pltpu.roll(value, i + 1, 2), packed)
        return jnp.where(
            lane == cz // 2 + i, pltpu.roll(value, cz // 2 + i, 2), packed
        )

    def load(c, i):
        fs = pl.ds(c * CHUNK, CHUNK)
        pair = ((fields_hbm, fields_ref), (source_hbm, source_ref))[i]
        return pltpu.make_async_copy(
            pair[0].at[fs], pair[1].at[fs], load_sem.at[i, c]
        )

    load_vel = pltpu.make_async_copy(vel_hbm, vel_ref, once_sem.at[0])
    load_diff = pltpu.make_async_copy(diff_hbm, diff_ref, once_sem.at[1])

    for d, ref in enumerate((xlo, xhi, ylo, yhi, zlo, zhi)):

        @pl.when(jnp.logical_not(receives(d)))
        def _(ref=ref):
            ref[...] = jnp.zeros_like(ref)

    barrier = pltpu.get_barrier_semaphore()
    for d in range(6):

        @pl.when(sends(d))
        def _(d=d):
            pl.semaphore_signal(
                barrier, inc=1, device_id=target(d), device_id_type=MESH
            )

    for c in range(chunks):
        load(c, 0).start()
    load_vel.start()
    load_diff.start()
    for c in range(chunks):
        load(c, 1).start()
    arriving = sum(receives(d).astype(jnp.int32) for d in range(6))
    pl.semaphore_wait(barrier, arriving)

    def first(c, _):
        for d in range(2):
            start(0, c, d)
        return 0

    lax.fori_loop(0, chunks, first, 0)

    def first_yz(c, _):
        load(c, 0).wait()
        for d in (2, 3):
            start(0, c, d)
        packed = jnp.zeros((cx, cy, cz), jnp.float32)
        for i in range(CHUNK):
            packed = pack_z(fields_ref[c * CHUNK + i], i, packed)
        zsend[0, c] = packed
        for d in (4, 5):
            start(0, c, d)
        return 0

    lax.fori_loop(0, chunks, first_yz, 0)

    load_vel.wait()
    load_diff.wait()
    total = jnp.ones((cx, cy, cz), jnp.float32)
    for a in range(3):
        up = COURANT * jnp.maximum(vel_ref[a], 0.0)
        down = -COURANT * jnp.minimum(vel_ref[a], 0.0)
        coef[2 * a] = up
        coef[2 * a + 1] = down
        total = total - up - down
    coef[6] = total
    plan_ref[...] = jnp.broadcast_to(
        ordered(reacting_ref[...] * counts_ref[...]), plan_ref.shape
    )

    row = lax.broadcasted_iota(jnp.int32, (cy, cz), 0)
    col = lax.broadcasted_iota(jnp.int32, (cy, cz), 1)

    def substep(step):
        src = fields_ref if step == 0 else mid_ref
        dst = mid_ref if step == 0 else out_ref

        def chunk(c, _):
            if step == 0:
                load(c, 1).wait()
            for d in range(6):

                @pl.when(receives(d))
                def _(d=d):
                    copy(step, c, d).wait_recv()

            def one(i, _):
                f = c * CHUNK + i
                diffuse = diff_ref[f]
                for x in range(cx):
                    here = src[f, x]
                    x_dn = src[f, x - 1] if x > 0 else xlo[step, f]
                    x_up = src[f, x + 1] if x < cx - 1 else xhi[step, f]
                    y_dn = jnp.where(
                        row == 0, ylo[step, f, pl.ds(x, 1)], pltpu.roll(here, 1, 0)
                    )
                    y_up = jnp.where(
                        row == cy - 1,
                        yhi[step, f, pl.ds(x, 1)],
                        pltpu.roll(here, cy - 1, 0),
                    )
                    z_dn = jnp.where(
                        col == 0,
                        pltpu.roll(zlo[step, c, x], lax.rem(cz - i, cz), 1),
                        pltpu.roll(here, 1, 1),
                    )
                    z_up = jnp.where(
                        col == cz - 1,
                        pltpu.roll(zhi[step, c, x], cz // 2 - 1 - i, 1),
                        pltpu.roll(here, cz - 1, 1),
                    )
                    flow = here * coef[6, x]
                    around = here * -6.0
                    for a, (dn, up) in enumerate(
                        ((x_dn, x_up), (y_dn, y_up), (z_dn, z_up))
                    ):
                        flow = flow + (dn * coef[2 * a, x] + up * coef[2 * a + 1, x])
                        around = around + (dn + up)
                    dst[f, x] = source_ref[f, x] + flow + diffuse * around
                return 0

            lax.fori_loop(0, CHUNK, one, 0)
            if step == 0:
                packed = jnp.zeros((cx, cy, cz), jnp.float32)
                for i in range(CHUNK):
                    packed = pack_z(mid_ref[c * CHUNK + i], i, packed)
                zsend[1, c] = packed
                for d in range(6):
                    start(1, c, d)
            return 0

        lax.fori_loop(0, chunks, chunk, 0)

    substep(0)
    substep(1)

    def finish(c, _):
        for step in range(2):
            for d in range(6):

                @pl.when(sends(d))
                def _(d=d, step=step):
                    copy(step, c, d).wait_send()

        return 0

    lax.fori_loop(0, chunks, finish, 0)


def transport(fields, source, velocity, diffusivity, reacting, counts):
    nf, cx, cy, cz = fields.shape
    chunks = nf // CHUNK
    sizes = tuple(lax.axis_size(a) for a in ("gx", "gy", "gz"))
    f32 = jnp.float32
    vmem = pl.BlockSpec(memory_space=pltpu.VMEM)
    return pl.pallas_call(
        functools.partial(transport_kernel, sizes),
        out_shape=(
            jax.ShapeDtypeStruct(fields.shape, f32),
            jax.ShapeDtypeStruct((8, cx * cy), jnp.int32),
        ),
        in_specs=[pl.BlockSpec(memory_space=pl.ANY)] * 4 + [vmem, vmem],
        out_specs=(vmem, vmem),
        scratch_shapes=[
            pltpu.SMEM((nf,), f32),
            pltpu.VMEM((nf, cx, cy, cz), f32),
            pltpu.VMEM((nf, cx, cy, cz), f32),
            pltpu.VMEM(velocity.shape, f32),
            pltpu.VMEM((nf, cx, cy, cz), f32),
            pltpu.VMEM((7, cx, cy, cz), f32),
            pltpu.VMEM((2, nf, cy, cz), f32),
            pltpu.VMEM((2, nf, cy, cz), f32),
            pltpu.VMEM((2, nf, cx, cz), f32),
            pltpu.VMEM((2, nf, cx, cz), f32),
            pltpu.VMEM((2, chunks, cx, cy, cz), f32),
            pltpu.VMEM((2, chunks, cx, cy, cz), f32),
            pltpu.VMEM((2, chunks, cx, cy, cz), f32),
            pltpu.SemaphoreType.DMA((2, chunks, 6)),
            pltpu.SemaphoreType.DMA((2, chunks, 6)),
            pltpu.SemaphoreType.DMA((2, chunks)),
            pltpu.SemaphoreType.DMA((2,)),
        ],
        compiler_params=pltpu.CompilerParams(
            collective_id=0, has_side_effects=True, vmem_limit_bytes=60 * 2**20
        ),
    )(
        diffusivity,
        fields,
        source,
        velocity,
        reacting.reshape(cx, cy),
        counts.reshape(cx, cy),
    )


def halves(value):
    hi = value.astype(jnp.bfloat16).astype(jnp.float32)
    return hi, value - hi


def chemistry_kernel(
    reactions,
    plan_ref,
    mech_ref,
    pre_ref,
    act_ref,
    heat_ref,
    state_ref,
    out_ref,
    wide_ref,
    gather_ref,
    scatter_ref,
):
    blocks = plan_ref.shape[1]
    lanes = wide_ref.shape[1]
    reac = gather_ref.shape[0]
    rows = scatter_ref.shape[0] // 2
    species = rows - 2
    out_ref[...] = state_ref[...]

    sub = lax.broadcasted_iota(jnp.int32, (rows, lanes), 0)
    wide_ref[...] = jnp.ones_like(wide_ref)
    wide_ref[pl.ds(0, 4), pl.ds(0, reactions)] = mech_ref[...].astype(jnp.float32)
    for i, ref in enumerate((act_ref, pre_ref, heat_ref)):
        wide_ref[pl.ds(4 + i, 1), pl.ds(0, reactions)] = ref[...]
    ids = sub.astype(jnp.float32)
    hot = [(wide_ref[pl.ds(i, 1), :] == ids).astype(jnp.float32) for i in range(4)]
    act_hi, act_lo = halves(wide_ref[pl.ds(4, 1), :] * -math.log2(math.e))
    real = lax.broadcasted_iota(jnp.int32, (1, lanes), 1) < reactions
    pre = jnp.where(real, jnp.log2(wide_ref[pl.ds(5, 1), :]), -3e4)
    pre_hi, pre_lo = halves(pre)
    heat_hi, heat_lo = halves(wide_ref[pl.ds(6, 1), :])

    def with_rows(base, one, two):
        base = jnp.where(sub == species, one, base)
        return jnp.where(sub == species + 1, two, base)

    used = hot[0] + hot[1]
    none = jnp.zeros((rows, lanes), jnp.float32)
    turned = jnp.concatenate(
        [
            with_rows(used, act_hi, pre_hi),
            with_rows(used, act_hi, 0.0),
            with_rows(none, act_lo, pre_lo),
            jnp.zeros((lanes - 3 * rows, lanes), jnp.float32),
        ],
        0,
    ).T
    gather_ref[...] = turned[:reac, : 3 * rows].astype(jnp.bfloat16)
    made = with_rows(hot[2] + hot[3], heat_hi, heat_lo)
    table = jnp.concatenate([used, made], 0)[:, :reac]
    scatter_ref[...] = jnp.concatenate([table, table], 1).astype(jnp.bfloat16)

    width = state_ref.shape[1]

    def group(g, _):
        codes = [plan_ref[0, g * GROUP + i] for i in range(GROUP)]
        ids = [lax.rem(code, blocks) for code in codes]
        ns = [lax.div(code, blocks) for code in codes]
        state = jnp.concatenate(
            [out_ref[pl.ds(b, rows, stride=blocks), :] for b in ids], 1
        )
        count = jnp.concatenate([jnp.full((rows, width), n, jnp.int32) for n in ns], 1)
        wide = CHEM_STEP / jnp.maximum(count, 1).astype(jnp.float32)
        rid = lax.broadcasted_iota(jnp.int32, (rows, GROUP * width), 0)

        def step(s, y):
            logs = jnp.where(rid == species, 1.0 / y, jnp.log2(y))
            hi, lo = halves(jnp.where(rid == species + 1, 1.0, logs))
            q = jnp.exp2(
                jnp.dot(
                    gather_ref[...],
                    jnp.concatenate([hi, lo, hi], 0).astype(jnp.bfloat16),
                    preferred_element_type=jnp.float32,
                )
            )
            q_hi = q.astype(jnp.bfloat16)
            q_lo = (q - q_hi.astype(jnp.float32)).astype(jnp.bfloat16)
            sums = jnp.dot(
                scatter_ref[...],
                jnp.concatenate([q_hi, q_lo], 0),
                preferred_element_type=jnp.float32,
            )
            loss = sums[:rows]
            gain = sums[rows:]
            fresh = (y + wide * gain) * (y / (y + wide * loss))
            warm = y[species : species + 1] + wide[:1] * (
                gain[species : species + 1] + gain[species + 1 : species + 2]
            )
            fresh = jnp.where(rid == species, warm, fresh)
            keep = jnp.logical_or(rid == species + 1, s >= count)
            return jnp.where(keep, y, fresh)

        most = ns[0]
        for n in ns[1:]:
            most = jnp.maximum(most, n)
        state = lax.fori_loop(0, most, step, state)
        for i, b in enumerate(ids):
            out_ref[pl.ds(b, rows, stride=blocks), :] = state[
                :, i * width : (i + 1) * width
            ]
        return 0

    def busy(g):
        return jnp.logical_and(
            g < blocks // GROUP,
            plan_ref[0, jnp.minimum(g * GROUP, blocks - 1)] >= blocks,
        )

    lax.while_loop(busy, lambda g: (group(g, 0), g + 1)[1], 0)


def chemistry(state, plan, mechanism, prefactor, activation, heat_release):
    nf, cx, cy, cz = state.shape
    blocks = cx * cy
    reactions = prefactor.shape[0]
    lanes = 128
    reac = -(-reactions // 16) * 16
    rows = 24
    vmem = pl.BlockSpec(memory_space=pltpu.VMEM)
    smem = pl.BlockSpec(memory_space=pltpu.SMEM)
    flat = state.reshape(nf * blocks, cz)
    out = pl.pallas_call(
        functools.partial(chemistry_kernel, reactions),
        out_shape=jax.ShapeDtypeStruct(flat.shape, jnp.float32),
        in_specs=[smem] + [vmem] * 5,
        out_specs=vmem,
        scratch_shapes=[
            pltpu.VMEM((8, lanes), jnp.float32),
            pltpu.VMEM((reac, 3 * rows), jnp.bfloat16),
            pltpu.VMEM((2 * rows, 2 * reac), jnp.bfloat16),
        ],
        compiler_params=pltpu.CompilerParams(vmem_limit_bytes=48 * 2**20),
    )(
        plan,
        mechanism,
        prefactor.reshape(1, reactions),
        activation.reshape(1, reactions),
        heat_release.reshape(1, reactions),
        flat,
    )
    return out.reshape(state.shape)


def body(
    fields,
    source,
    velocity,
    diffusivity,
    reacting,
    counts,
    mechanism,
    prefactor,
    activation,
    heat_release,
):
    moved, plan = transport(
        fields, source, velocity, diffusivity, reacting, counts
    )
    return chemistry(moved, plan, mechanism, prefactor, activation, heat_release)


def solution(mesh):
    grid = P(None, "gx", "gy", "gz")
    placed = (grid, grid, grid, P(), P("gx", "gy", "gz"), P("gx", "gy", "gz"))
    return jax.shard_map(
        body,
        mesh=mesh,
        in_specs=placed + (P(),) * 4,
        out_specs=grid,
        check_vma=False,
    )
```

```python
import functools
import math

import jax
import jax.numpy as jnp
from jax import lax
from jax.experimental import pallas as pl
from jax.experimental.pallas import tpu as pltpu
from jax.sharding import PartitionSpec as P

COURANT = 0.15
CHEM_STEP = 0.25
CHUNK = 8
GROUP = 32
MESH = pl.DeviceIdType.MESH


def ordered(todo):
    cx, cy = todo.shape
    blocks = cx * cy
    f32 = jnp.float32
    wide = jnp.concatenate([todo.astype(f32)] * cx, 1)
    shape = (cx, blocks)
    mine = lax.broadcasted_iota(jnp.int32, shape, 1) // cy == lax.broadcasted_iota(
        jnp.int32, shape, 0
    )
    row = jnp.sum(jnp.where(mine, wide, 0.0), 0, keepdims=True)
    down = lax.broadcasted_iota(jnp.int32, (blocks, blocks), 0)
    along = lax.broadcasted_iota(jnp.int32, (blocks, blocks), 1)
    col = jnp.sum(jnp.where(down == along, row, 0.0), 1, keepdims=True)
    ahead = (row > col) | ((row == col) & (along < down))
    rank = jnp.sum(jnp.where(ahead, 1.0, 0.0), 1, keepdims=True)
    value = down.astype(f32) + blocks * col
    placed = rank == along.astype(f32)
    return jnp.sum(jnp.where(placed, value, 0.0), 0, keepdims=True).astype(jnp.int32)


def transport_kernel(
    sizes,
    diff_hbm,
    fields_hbm,
    source_hbm,
    vel_hbm,
    reacting_ref,
    counts_ref,
    out_ref,
    plan_ref,
    diff_ref,
    fields_ref,
    source_ref,
    vel_ref,
    mid_ref,
    coef,
    xlo,
    xhi,
    ylo,
    yhi,
    zlo,
    zhi,
    zsend,
    send_sem,
    recv_sem,
    load_sem,
    once_sem,
):
    nf, cx, cy, cz = fields_hbm.shape
    chunks = nf // CHUNK
    axes = ("gx", "gy", "gz")
    where = [lax.axis_index(a) for a in axes]
    has_prev = [w > 0 for w in where]
    has_next = [w < n - 1 for w, n in zip(where, sizes)]

    def target(d):
        a = d // 2
        return {axes[a]: where[a] + (1 if d % 2 == 0 else -1)}

    def sends(d):
        return has_next[d // 2] if d % 2 == 0 else has_prev[d // 2]

    def receives(d):
        return has_prev[d // 2] if d % 2 == 0 else has_next[d // 2]

    def copy(step, c, d):
        src = fields_ref if step == 0 else mid_ref
        if step == 0 and d < 2:
            src = fields_hbm
        fs = pl.ds(c * CHUNK, CHUNK)
        if d == 0:
            pair = (src.at[fs, cx - 1], xlo.at[step, fs])
        elif d == 1:
            pair = (src.at[fs, 0], xhi.at[step, fs])
        elif d == 2:
            pair = (src.at[fs, :, cy - 1], ylo.at[step, fs])
        elif d == 3:
            pair = (src.at[fs, :, 0], yhi.at[step, fs])
        elif d == 4:
            pair = (zsend.at[step, c], zlo.at[step, c])
        else:
            pair = (zsend.at[step, c], zhi.at[step, c])
        return pltpu.make_async_remote_copy(
            src_ref=pair[0],
            dst_ref=pair[1],
            send_sem=send_sem.at[step, c, d],
            recv_sem=recv_sem.at[step, c, d],
            device_id=target(d),
            device_id_type=MESH,
        )

    def start(step, c, d):
        @pl.when(sends(d))
        def _():
            copy(step, c, d).start()

    lane = lax.broadcasted_iota(jnp.int32, (cx, cy, cz), 2)

    def pack_z(value, i, packed):
        packed = jnp.where(lane == i, pltpu.roll(value, i + 1, 2), packed)
        return jnp.where(
            lane == cz // 2 + i, pltpu.roll(value, cz // 2 + i, 2), packed
        )

    def load(c, i):
        fs = pl.ds(c * CHUNK, CHUNK)
        pair = ((fields_hbm, fields_ref), (source_hbm, source_ref))[i]
        return pltpu.make_async_copy(
            pair[0].at[fs], pair[1].at[fs], load_sem.at[i, c]
        )

    load_vel = pltpu.make_async_copy(vel_hbm, vel_ref, once_sem.at[0])
    load_diff = pltpu.make_async_copy(diff_hbm, diff_ref, once_sem.at[1])

    for d, ref in enumerate((xlo, xhi, ylo, yhi, zlo, zhi)):

        @pl.when(jnp.logical_not(receives(d)))
        def _(ref=ref):
            ref[...] = jnp.zeros_like(ref)

    barrier = pltpu.get_barrier_semaphore()
    for d in range(6):

        @pl.when(sends(d))
        def _(d=d):
            pl.semaphore_signal(
                barrier, inc=1, device_id=target(d), device_id_type=MESH
            )

    for c in range(chunks):
        load(c, 0).start()
    load_vel.start()
    load_diff.start()
    for c in range(chunks):
        load(c, 1).start()
    arriving = sum(receives(d).astype(jnp.int32) for d in range(6))
    pl.semaphore_wait(barrier, arriving)

    def first(c, _):
        for d in range(2):
            start(0, c, d)
        return 0

    lax.fori_loop(0, chunks, first, 0)

    def first_yz(c, _):
        load(c, 0).wait()
        for d in (2, 3):
            start(0, c, d)
        packed = jnp.zeros((cx, cy, cz), jnp.float32)
        for i in range(CHUNK):
            packed = pack_z(fields_ref[c * CHUNK + i], i, packed)
        zsend[0, c] = packed
        for d in (4, 5):
            start(0, c, d)
        return 0

    lax.fori_loop(0, chunks, first_yz, 0)

    load_vel.wait()
    load_diff.wait()
    total = jnp.ones((cx, cy, cz), jnp.float32)
    for a in range(3):
        up = COURANT * jnp.maximum(vel_ref[a], 0.0)
        down = -COURANT * jnp.minimum(vel_ref[a], 0.0)
        coef[2 * a] = up
        coef[2 * a + 1] = down
        total = total - up - down
    coef[6] = total
    plan_ref[...] = jnp.broadcast_to(
        ordered(reacting_ref[...] * counts_ref[...]), plan_ref.shape
    )

    row = lax.broadcasted_iota(jnp.int32, (cy, cz), 0)
    col = lax.broadcasted_iota(jnp.int32, (cy, cz), 1)

    def substep(step):
        src = fields_ref if step == 0 else mid_ref
        dst = mid_ref if step == 0 else out_ref

        def chunk(c, _):
            if step == 0:
                load(c, 1).wait()
            for d in range(6):

                @pl.when(receives(d))
                def _(d=d):
                    copy(step, c, d).wait_recv()

            def one(i, _):
                f = c * CHUNK + i
                diffuse = diff_ref[f]
                for x in range(cx):
                    here = src[f, x]
                    x_dn = src[f, x - 1] if x > 0 else xlo[step, f]
                    x_up = src[f, x + 1] if x < cx - 1 else xhi[step, f]
                    y_dn = jnp.where(
                        row == 0, ylo[step, f, pl.ds(x, 1)], pltpu.roll(here, 1, 0)
                    )
                    y_up = jnp.where(
                        row == cy - 1,
                        yhi[step, f, pl.ds(x, 1)],
                        pltpu.roll(here, cy - 1, 0),
                    )
                    z_dn = jnp.where(
                        col == 0,
                        pltpu.roll(zlo[step, c, x], lax.rem(cz - i, cz), 1),
                        pltpu.roll(here, 1, 1),
                    )
                    z_up = jnp.where(
                        col == cz - 1,
                        pltpu.roll(zhi[step, c, x], cz // 2 - 1 - i, 1),
                        pltpu.roll(here, cz - 1, 1),
                    )
                    flow = here * coef[6, x]
                    around = here * -6.0
                    for a, (dn, up) in enumerate(
                        ((x_dn, x_up), (y_dn, y_up), (z_dn, z_up))
                    ):
                        flow = flow + (dn * coef[2 * a, x] + up * coef[2 * a + 1, x])
                        around = around + (dn + up)
                    dst[f, x] = source_ref[f, x] + flow + diffuse * around
                return 0

            lax.fori_loop(0, CHUNK, one, 0)
            if step == 0:
                packed = jnp.zeros((cx, cy, cz), jnp.float32)
                for i in range(CHUNK):
                    packed = pack_z(mid_ref[c * CHUNK + i], i, packed)
                zsend[1, c] = packed
                for d in range(6):
                    start(1, c, d)
            return 0

        lax.fori_loop(0, chunks, chunk, 0)

    substep(0)
    substep(1)

    def finish(c, _):
        for step in range(2):
            for d in range(6):

                @pl.when(sends(d))
                def _(d=d, step=step):
                    copy(step, c, d).wait_send()

        return 0

    lax.fori_loop(0, chunks, finish, 0)


def transport(fields, source, velocity, diffusivity, reacting, counts):
    nf, cx, cy, cz = fields.shape
    chunks = nf // CHUNK
    sizes = tuple(lax.axis_size(a) for a in ("gx", "gy", "gz"))
    f32 = jnp.float32
    vmem = pl.BlockSpec(memory_space=pltpu.VMEM)
    return pl.pallas_call(
        functools.partial(transport_kernel, sizes),
        out_shape=(
            jax.ShapeDtypeStruct(fields.shape, f32),
            jax.ShapeDtypeStruct((8, cx * cy), jnp.int32),
        ),
        in_specs=[pl.BlockSpec(memory_space=pl.ANY)] * 4 + [vmem, vmem],
        out_specs=(vmem, vmem),
        scratch_shapes=[
            pltpu.SMEM((nf,), f32),
            pltpu.VMEM((nf, cx, cy, cz), f32),
            pltpu.VMEM((nf, cx, cy, cz), f32),
            pltpu.VMEM(velocity.shape, f32),
            pltpu.VMEM((nf, cx, cy, cz), f32),
            pltpu.VMEM((7, cx, cy, cz), f32),
            pltpu.VMEM((2, nf, cy, cz), f32),
            pltpu.VMEM((2, nf, cy, cz), f32),
            pltpu.VMEM((2, nf, cx, cz), f32),
            pltpu.VMEM((2, nf, cx, cz), f32),
            pltpu.VMEM((2, chunks, cx, cy, cz), f32),
            pltpu.VMEM((2, chunks, cx, cy, cz), f32),
            pltpu.VMEM((2, chunks, cx, cy, cz), f32),
            pltpu.SemaphoreType.DMA((2, chunks, 6)),
            pltpu.SemaphoreType.DMA((2, chunks, 6)),
            pltpu.SemaphoreType.DMA((2, chunks)),
            pltpu.SemaphoreType.DMA((2,)),
        ],
        compiler_params=pltpu.CompilerParams(
            collective_id=0, has_side_effects=True, vmem_limit_bytes=60 * 2**20
        ),
    )(
        diffusivity,
        fields,
        source,
        velocity,
        reacting.reshape(cx, cy),
        counts.reshape(cx, cy),
    )


def halves(value):
    hi = value.astype(jnp.bfloat16).astype(jnp.float32)
    return hi, value - hi


def chemistry_kernel(
    reactions,
    mech_ref,
    pre_ref,
    act_ref,
    heat_ref,
    plan_hbm,
    state_hbm,
    out_hbm,
    plan_ref,
    out_ref,
    wide_ref,
    gather_ref,
    scatter_ref,
    sems,
):
    blocks = plan_ref.shape[1]
    lanes = wide_ref.shape[1]
    reac = gather_ref.shape[0]
    rows = scatter_ref.shape[0] // 2
    species = rows - 2
    ours = pl.ds(0, out_ref.shape[0])
    others = pl.ds(out_ref.shape[0], state_hbm.shape[0] - out_ref.shape[0])
    load_plan = pltpu.make_async_copy(plan_hbm, plan_ref, sems.at[0])
    load = pltpu.make_async_copy(state_hbm.at[ours], out_ref, sems.at[1])
    pass_on = pltpu.make_async_copy(
        state_hbm.at[others], out_hbm.at[others], sems.at[2]
    )
    store = pltpu.make_async_copy(out_ref, out_hbm.at[ours], sems.at[3])
    load_plan.start()
    load.start()
    pass_on.start()

    sub = lax.broadcasted_iota(jnp.int32, (rows, lanes), 0)
    wide_ref[...] = jnp.ones_like(wide_ref)
    wide_ref[pl.ds(0, 4), pl.ds(0, reactions)] = mech_ref[...].astype(jnp.float32)
    for i, ref in enumerate((act_ref, pre_ref, heat_ref)):
        wide_ref[pl.ds(4 + i, 1), pl.ds(0, reactions)] = ref[...]
    ids = sub.astype(jnp.float32)
    hot = [(wide_ref[pl.ds(i, 1), :] == ids).astype(jnp.float32) for i in range(4)]
    act_hi, act_lo = halves(wide_ref[pl.ds(4, 1), :] * -math.log2(math.e))
    real = lax.broadcasted_iota(jnp.int32, (1, lanes), 1) < reactions
    pre = jnp.where(real, jnp.log2(wide_ref[pl.ds(5, 1), :]), -3e4)
    pre_hi, pre_lo = halves(pre)
    heat_hi, heat_lo = halves(wide_ref[pl.ds(6, 1), :])

    def with_rows(base, one, two):
        base = jnp.where(sub == species, one, base)
        return jnp.where(sub == species + 1, two, base)

    used = hot[0] + hot[1]
    none = jnp.zeros((rows, lanes), jnp.float32)
    turned = jnp.concatenate(
        [
            with_rows(used, act_hi, pre_hi),
            with_rows(used, act_hi, 0.0),
            with_rows(none, act_lo, pre_lo),
            jnp.zeros((lanes - 3 * rows, lanes), jnp.float32),
        ],
        0,
    ).T
    gather_ref[...] = turned[:reac, : 3 * rows].astype(jnp.bfloat16)
    made = with_rows(hot[2] + hot[3], heat_hi, heat_lo)
    table = jnp.concatenate([used, made], 0)[:, :reac]
    scatter_ref[...] = jnp.concatenate([table, table], 1).astype(jnp.bfloat16)

    width = out_ref.shape[1]
    load_plan.wait()
    load.wait()

    def group(g, _):
        codes = [plan_ref[0, g * GROUP + i] for i in range(GROUP)]
        ids = [lax.rem(code, blocks) for code in codes]
        ns = [lax.div(code, blocks) for code in codes]
        state = jnp.concatenate(
            [out_ref[pl.ds(b, rows, stride=blocks), :] for b in ids], 1
        )
        count = jnp.concatenate([jnp.full((rows, width), n, jnp.int32) for n in ns], 1)
        wide = CHEM_STEP / jnp.maximum(count, 1).astype(jnp.float32)
        rid = lax.broadcasted_iota(jnp.int32, (rows, GROUP * width), 0)

        def step(s, y):
            logs = jnp.where(rid == species, 1.0 / y, jnp.log2(y))
            hi, lo = halves(jnp.where(rid == species + 1, 1.0, logs))
            q = jnp.exp2(
                jnp.dot(
                    gather_ref[...],
                    jnp.concatenate([hi, lo, hi], 0).astype(jnp.bfloat16),
                    preferred_element_type=jnp.float32,
                )
            )
            q_hi = q.astype(jnp.bfloat16)
            q_lo = (q - q_hi.astype(jnp.float32)).astype(jnp.bfloat16)
            sums = jnp.dot(
                scatter_ref[...],
                jnp.concatenate([q_hi, q_lo], 0),
                preferred_element_type=jnp.float32,
            )
            loss = sums[:rows]
            gain = sums[rows:]
            fresh = (y + wide * gain) * (y / (y + wide * loss))
            warm = y[species : species + 1] + wide[:1] * (
                gain[species : species + 1] + gain[species + 1 : species + 2]
            )
            fresh = jnp.where(rid == species, warm, fresh)
            keep = jnp.logical_or(rid == species + 1, s >= count)
            return jnp.where(keep, y, fresh)

        most = ns[0]
        for n in ns[1:]:
            most = jnp.maximum(most, n)
        state = lax.fori_loop(0, most, step, state)
        for i, b in enumerate(ids):
            out_ref[pl.ds(b, rows, stride=blocks), :] = state[
                :, i * width : (i + 1) * width
            ]
        return 0

    def busy(g):
        return jnp.logical_and(
            g < blocks // GROUP,
            plan_ref[0, jnp.minimum(g * GROUP, blocks - 1)] >= blocks,
        )

    lax.while_loop(busy, lambda g: (group(g, 0), g + 1)[1], 0)
    store.start()
    store.wait()
    pass_on.wait()


def chemistry(state, plan, mechanism, prefactor, activation, heat_release):
    nf, cx, cy, cz = state.shape
    blocks = cx * cy
    reactions = prefactor.shape[0]
    lanes = 128
    reac = -(-reactions // 16) * 16
    rows = 24
    vmem = pl.BlockSpec(memory_space=pltpu.VMEM)
    hbm = pl.BlockSpec(memory_space=pl.ANY)
    flat = state.reshape(nf * blocks, cz)
    out = pl.pallas_call(
        functools.partial(chemistry_kernel, reactions),
        out_shape=jax.ShapeDtypeStruct(flat.shape, jnp.float32),
        in_specs=[vmem] * 4 + [hbm] * 2,
        out_specs=hbm,
        scratch_shapes=[
            pltpu.SMEM(plan.shape, jnp.int32),
            pltpu.VMEM((rows * blocks, cz), jnp.float32),
            pltpu.VMEM((8, lanes), jnp.float32),
            pltpu.VMEM((reac, 3 * rows), jnp.bfloat16),
            pltpu.VMEM((2 * rows, 2 * reac), jnp.bfloat16),
            pltpu.SemaphoreType.DMA((4,)),
        ],
        compiler_params=pltpu.CompilerParams(vmem_limit_bytes=60 * 2**20),
    )(
        mechanism,
        prefactor.reshape(1, reactions),
        activation.reshape(1, reactions),
        heat_release.reshape(1, reactions),
        plan,
        flat,
    )
    return out.reshape(state.shape)


def body(
    fields,
    source,
    velocity,
    diffusivity,
    reacting,
    counts,
    mechanism,
    prefactor,
    activation,
    heat_release,
):
    moved, plan = transport(
        fields, source, velocity, diffusivity, reacting, counts
    )
    return chemistry(moved, plan, mechanism, prefactor, activation, heat_release)


def solution(mesh):
    grid = P(None, "gx", "gy", "gz")
    placed = (grid, grid, grid, P(), P("gx", "gy", "gz"), P("gx", "gy", "gz"))
    return jax.shard_map(
        body,
        mesh=mesh,
        in_specs=placed + (P(),) * 4,
        out_specs=grid,
        check_vma=False,
    )
```
